256 devices in a mesh: row: 16 (over x_hi, y, core), col: 16 (over z, x_lo).
Axes of the slice: x: 4 (x_hi: 2, x_lo: 2; x = x_hi * 2 + x_lo), y: 4, z: 8, core: 2. Of those that a mesh axis runs over, the one named last changes fastest.
Arguments:
- basis: float32 [4096, 6144], P('row', 'col'), may hold values from -0.625 to 0.625
- image: float32 [4096, 6144], P('row', 'col'), may hold values from -0.625 to 0.625
- coeffs: float32 [6144, 4096], P('row', 'col'), may hold values from -6 to 6
Outputs:
- gram: float32 [6144, 6144], P('row', 'col')
- stiffness: float32 [6144, 6144], P('row', 'col')
- rotated: float32 [4096, 4096], P('row', 'col')
The draws below stay inside these ranges and needn't reach their ends.
All inputs are finite; a program needn't handle non-finite values.
Results may differ from the reference program's by a relative error of at most 0.00007.
Values sent between devices are 32-bit elements; how exact they have to be, the bound alone decides.
A program may use at most 128 MiB of HBM per device.

```python
import jax
import jax.numpy as jnp
from jax import lax

NEV = 2048
ROWS_DEV = 256
ROWS = 4096
WIDTH = 6144
NOUT = 4096
N_ROW = 16


def strengthened(values, rng, source, target, shards_of, factor):
    def block_of(axis_at):
        return (jnp.arange(values.shape[axis_at]) // (values.shape[axis_at] // shards_of)).reshape((-1,) + (1,) * (values.ndim - 1 - axis_at))

    first = jax.random.permutation(rng, shards_of)[block_of(target)]
    second = (block_of(target) + shards_of // 2) % shards_of
    return jnp.where((block_of(source) == first) | (block_of(source) == second), factor * values, values)


def steps_of(own_key, extent, split, least, top_value):
    gain = 1.0
    for axis_at, blocks in split:
        steps = jax.random.uniform(jax.random.fold_in(jax.random.fold_in(own_key, 6), axis_at), (blocks,), jnp.float32, least / len(split), top_value / len(split))
        gain = gain * jnp.repeat(jnp.exp(steps), extent[axis_at] // blocks).reshape((-1,) + (1,) * (len(extent) - 1 - axis_at))
    return gain


def normal_values(rng, dims, width, bound, pieces=(), dtype=jnp.bfloat16):
    entries = width * jax.random.normal(rng, dims, jnp.float32)
    if pieces:
        entries = entries * steps_of(rng, dims, pieces, -0.22, 0.18)
    return jnp.clip(entries, -bound, bound).astype(dtype)


def heavy_noise(own_key, extent, width, most, cuts, heavy, dtype=jnp.bfloat16):
    drawn = width * jax.random.normal(own_key, extent, jnp.float32)
    if cuts:
        drawn = drawn * steps_of(own_key, extent, cuts, -0.22, 0.18)
    return jnp.clip(strengthened(drawn, jax.random.fold_in(own_key, 3), *heavy), -most, most).astype(dtype)


def setup_inputs(seed: int = 0) -> dict:
    seeds = jax.random.split(jax.random.key(seed), 4)
    return {
        "basis": heavy_noise(seeds[0], (ROWS, WIDTH), (2.0 * (ROWS_DEV * N_ROW) ** -0.5), 0.625, ((0, 16), (1, 16)), (0, 1, 16, 2.0), jnp.float32),
        "image": heavy_noise(seeds[1], (ROWS, WIDTH), (2.0 * (ROWS_DEV * N_ROW) ** -0.5), 0.625, ((0, 16), (1, 16)), (0, 1, 16, 2.0), jnp.float32),
        "coeffs": normal_values(seeds[2], (WIDTH, NOUT), (0.5 * (ROWS_DEV * N_ROW) ** 0.5 * (3 * NEV) ** -0.5), 6.0, ((0, 16), (1, 16)), jnp.float32),
    }


def reference(basis, image, coeffs):
    highest = lax.Precision.HIGHEST
    gram = jnp.dot(basis.T, basis, precision=highest, preferred_element_type=jnp.float32)
    stiffness = jnp.dot(basis.T, image, precision=highest, preferred_element_type=jnp.float32)
    rotated = jnp.dot(basis, coeffs, precision=highest, preferred_element_type=jnp.float32)
    return gram, stiffness, rotated
```

```python
import functools

import jax
import jax.numpy as jnp
from jax import lax
from jax.experimental import pallas as pl
from jax.experimental.pallas import tpu as pltpu
from jax.sharding import PartitionSpec as P

MESH = pl.DeviceIdType.MESH
F32, BF16 = jnp.float32, jnp.bfloat16
NY, NZ = 4, 8
RB, CB, OB = 256, 384, 256
NB = 8
NM, MW = 3, 128
STEPS = NM * NB
LAG = 2


def halves(v):
    hi = v.astype(BF16)
    return hi, (v - hi.astype(F32)).astype(BF16)


def dot(a, b):
    return jnp.dot(a, b, preferred_element_type=F32)


def kernel(
    basis, image, coeffs, gram, stiff, rot,
    lbuf, rbuf, rt_hi, rt_lo, cbuf, c_hi, c_lo, l_hi, l_lo, pbuf, precv, rotp, rotc, rots, roty,
    l_recv, l_send, z_send, r_recv, r_send, c_recv, c_send, p_recv, p_send, rc_recv, rc_send, ry_recv, ry_send,
):
    row, col = lax.axis_index("row"), lax.axis_index("col")
    xh, y, core = lax.div(row, 8), lax.rem(lax.div(row, 2), 4), lax.rem(row, 2)
    z, xl = lax.div(col, 2), lax.rem(col, 2)
    zs = lax.rem(z, 4)
    d = lax.rem(z - y + NZ, 4)
    own_blk = y * 2 + core

    def dev(dxh=0, dxl=0, dy=0, dz=0, dc=0):
        a, b = lax.rem(xh + dxh, 2), lax.rem(xl + dxl, 2)
        return (a * 8 + lax.rem(y + dy + NY, NY) * 2 + lax.rem(core + dc, 2), lax.rem(z + dz + NZ, NZ) * 2 + b)

    other_core, partner = dev(dc=1), dev(dxh=1)
    y_up, y_dn, z_up, z_dn = dev(dy=1), dev(dy=-1), dev(dz=1), dev(dz=-1)

    def send(src, dst, s, r, to):
        return pltpu.make_async_remote_copy(
            src_ref=src, dst_ref=dst, send_sem=s, recv_sem=r, device_id=to, device_id_type=MESH
        )

    def arrived(dst, r):
        send(dst, dst, l_send.at[0, 0], r, other_core).wait_recv()

    barrier = pltpu.get_barrier_semaphore()
    peers = [dev(dxl=a, dy=b, dc=c) for a in range(2) for b in range(4) for c in range(2) if a + b + c]
    peers += [z_up, z_dn, partner]
    for p in peers:
        pl.semaphore_signal(barrier, inc=1, device_id=p, device_id_type=MESH)
    pl.semaphore_wait(barrier, len(peers))

    def gather(m, a):
        to = (xh * 8 + zs * 2 + xl, z * 2 + lax.rem(xl + a, 2))
        return send(
            basis.at[:, pl.ds(m * MW, MW)], lbuf.at[m, 0, own_blk], l_send.at[m, a], l_recv.at[m, 0, own_blk], to
        )

    mine = (y == zs) & (core == xl)

    def gather_start(m):
        @pl.when(mine)
        def _():
            pltpu.make_async_copy(
                basis.at[:, pl.ds(m * MW, MW)], lbuf.at[m, 0, own_blk], l_recv.at[m, 0, own_blk]
            ).start()

        @pl.when(jnp.logical_not(mine))
        def _():
            gather(m, 0).start()

        gather(m, 1).start()

    for m in range(NM):
        gather_start(m)

    sends = []

    def r_go(arr, blk, to, src=None):
        cp = send(
            rbuf.at[arr, blk] if src is None else src, rbuf.at[arr, blk], r_send.at[len(sends)], r_recv.at[arr, blk], to
        )
        cp.start()
        sends.append(cp)

    for arr, src in enumerate((basis, image)):
        pltpu.make_async_copy(src, rbuf.at[arr, own_blk], r_recv.at[arr, own_blk]).start()
        r_go(arr, own_blk, y_up, src)
        r_go(arr, own_blk, y_dn, src)
        r_go(arr, own_blk, other_core, src)

    own_c = pltpu.make_async_copy(coeffs, cbuf.at[xh], c_send.at[1])
    own_c.start()
    c_cp = send(coeffs, cbuf.at[xh], c_send.at[0], c_recv, partner)
    c_cp.start()

    def blk_of(dy, c):
        return lax.rem(y + dy, NY) * 2 + c

    def chunk(i):
        m, j = lax.div(i, NB), lax.rem(i, NB)
        q, c = lax.div(j, 2), lax.rem(j, 2)
        dy = jnp.where(q == 2, 3, jnp.where(q == 3, 2, q))
        return m, c, blk_of(dy, c)

    def z_copy(i, slot, m, blk, up):
        if up:
            to, into = z_up, jnp.where(d == 3, 1, 0)
        else:
            to, into = z_dn, 1
        return send(
            lbuf.at[m, slot, blk], lbuf.at[m, into, blk], z_send.at[0 if up else 1, i], l_recv.at[m, into, blk], to
        )

    def step_a(i, wait):
        m, c, blk = chunk(i)
        if not wait:
            arrived(lbuf.at[m, 0, blk], l_recv.at[m, 0, blk])

        @pl.when((d < 3) | (c == 0))
        def _():
            cp = z_copy(i, 0, m, blk, True)
            cp.wait_send() if wait else cp.start()

        @pl.when(d == 0)
        def _():
            cp = z_copy(i, 0, m, blk, False)
            cp.wait_send() if wait else cp.start()

    def step_b(i, wait):
        m, c, blk = chunk(i)
        if not wait:
            arrived(lbuf.at[m, 1, blk], l_recv.at[m, 1, blk])

        @pl.when((d > 1) | ((d == 1) & (c == 1)))
        def _():
            cp = z_copy(i, 1, m, blk, False)
            cp.wait_send() if wait else cp.start()

    def step(t):
        ia, ib = t - LAG * d, t - LAG * (4 - d)

        @pl.when((ia >= 0) & (ia < STEPS))
        def _():
            step_a(ia, False)

        @pl.when((ib >= 0) & (ib < STEPS))
        def _():
            step_b(ib, False)

    def loop(lo, hi, body):
        def go(t, carry):
            body(t)
            return carry

        lax.fori_loop(lo, hi, go, 0)

    def transpose(blk):
        for arr in range(2):
            arrived(rbuf.at[arr, blk], r_recv.at[arr, blk])
            hi, lo = halves(rbuf[arr, blk].T)
            at = (pl.ds(arr * CB, CB), pl.ds(pl.multiple_of(blk * RB, RB), RB))
            rt_hi[at] = hi
            rt_lo[at] = lo

    own = jnp.where(lax.div(lax.rem(z - d + NZ, NZ), 4) == xh, 0, 1)
    h_a = jnp.where(own == 0, xh, 1 - xh)

    def split_l(m, blks):
        for b in blks:
            at = pl.ds(b * RB, RB)
            for slot in range(2):
                hi, lo = halves(lbuf[m, slot, b])
                l_hi[at, pl.ds(slot * MW, MW)] = hi
                l_lo[at, pl.ds(slot * MW, MW)] = lo

    def grams(m, arr):
        at = pl.ds(arr * CB, CB)
        acc = dot(rt_hi[at, :], l_hi[...]) + dot(rt_hi[at, :], l_lo[...]) + dot(rt_lo[at, :], l_hi[...])
        pbuf[m, :, at] = acc.T

    def p_copy(m):
        src = pbuf.at[m, pl.ds(pl.multiple_of((1 - own) * MW, MW), MW)]
        return send(src, precv.at[m], p_send.at[m], p_recv.at[m], partner)

    def rotate(m, b):
        at = pl.ds(b * RB, RB)
        a_hi, a_lo = l_hi[at, :], l_lo[at, :]
        acc = dot(a_hi, c_hi[m]) + dot(a_hi, c_lo[m]) + dot(a_lo, c_hi[m])
        rotp[b] = acc if m == 0 else rotp[b] + acc

    loop(0, 13, step)

    for arr in range(2):
        for dy in (1, 3):
            blk = blk_of(dy, core)
            arrived(rbuf.at[arr, blk], r_recv.at[arr, blk])
            r_go(arr, blk, other_core)
            if (arr, dy) == (0, 3):
                r_go(arr, blk, y_up)
            if (arr, dy) == (1, 1):
                r_go(arr, blk, y_dn)

    def transpose_ready(blk):
        for arr in range(2):
            hi, lo = halves(rbuf[arr, blk].T)
            at = (pl.ds(arr * CB, CB), pl.ds(pl.multiple_of(blk * RB, RB), RB))
            rt_hi[at] = hi
            rt_lo[at] = lo

    def with_step(t, *work):
        step(jnp.int32(t))
        for f in work:
            f()

    def split_c():
        own_c.wait()
        arrived(cbuf.at[1 - xh], c_recv)
        for m in range(NM):
            for slot in range(2):
                h = h_a if slot == 0 else 1 - h_a
                hi, lo = halves(cbuf[h, pl.ds(m * MW, MW), :])
                c_hi[m, pl.ds(slot * MW, MW), :] = hi
                c_lo[m, pl.ds(slot * MW, MW), :] = lo

    with_step(13, lambda: transpose(blk_of(0, core)))
    with_step(14, lambda: transpose(blk_of(0, 1 - core)))
    with_step(15, lambda: transpose_ready(blk_of(1, core)))
    with_step(16, lambda: transpose_ready(blk_of(3, core)))
    with_step(17, lambda: transpose(blk_of(1, 1 - core)))
    with_step(18, lambda: transpose(blk_of(3, 1 - core)))
    with_step(19, split_c)
    blk = blk_of(2, core)
    for arr in range(2):
        arrived(rbuf.at[arr, blk], r_recv.at[arr, blk])
        r_go(arr, blk, other_core)
    with_step(20, lambda: transpose_ready(blk))
    with_step(21, lambda: transpose(blk_of(2, 1 - core)))

    def rot_some(m, blks):
        for b in blks:
            rotate(m, b)

    with_step(22, lambda: split_l(0, range(8)))
    with_step(23, lambda: grams(0, 0))
    with_step(24, lambda: grams(0, 1), lambda: p_copy(0).start())
    with_step(25, lambda: rot_some(0, range(8)))
    with_step(26, lambda: split_l(1, range(8)))
    with_step(27, lambda: grams(1, 0))
    with_step(28, lambda: grams(1, 1), lambda: p_copy(1).start())
    with_step(29, lambda: rot_some(1, range(8)))
    loop(30, STEPS + 4 * LAG, step)

    split_l(2, range(8))
    rot_some(2, range(8))
    rc = [
        send(rotp.at[b * 2 + 1 - core], rotc.at[b], rc_send.at[b], rc_recv.at[b], other_core) for b in range(NY)
    ]
    for cp in rc:
        cp.start()
    grams(2, 0)
    grams(2, 1)
    p_copy(2).start()
    for cp in rc:
        cp.wait()
    for b in range(NY):
        rots[b] = rotp[b * 2 + core] + rotc[b]
    ry = []
    for o in (2, 1, 3):
        cp = send(rots.at[lax.rem(y + o, NY)], roty.at[o - 1], ry_send.at[o - 1], ry_recv.at[o - 1], dev(dy=o))
        cp.start()
        ry.append(cp)

    at_own = pl.ds(pl.multiple_of(own * MW, MW), MW)
    for m in range(NM):
        p_copy(m).wait()
        rows = pl.ds(m * MW, MW)
        gram[rows, :] = pbuf[m, at_own, pl.ds(0, CB)] + precv[m, :, pl.ds(0, CB)]
        stiff[rows, :] = pbuf[m, at_own, pl.ds(CB, CB)] + precv[m, :, pl.ds(CB, CB)]
    for cp in ry:
        cp.wait()
    rot[...] = rots[y] + roty[0] + roty[1] + roty[2]

    for m in range(NM):
        pl.when(jnp.logical_not(mine))(gather(m, 0).wait_send)
        gather(m, 1).wait_send()
    for cp in sends:
        cp.wait_send()
    c_cp.wait_send()

    def drain(i):
        step_a(i, True)
        step_b(i, True)

    loop(0, STEPS, drain)


def on_device(basis, image, coeffs):
    dma = pltpu.SemaphoreType.DMA
    return pl.pallas_call(
        kernel,
        out_shape=[
            jax.ShapeDtypeStruct((CB, CB), F32),
            jax.ShapeDtypeStruct((CB, CB), F32),
            jax.ShapeDtypeStruct((RB, OB), F32),
        ],
        in_specs=[pl.BlockSpec(memory_space=pltpu.VMEM)] * 3,
        out_specs=[pl.BlockSpec(memory_space=pltpu.VMEM)] * 3,
        scratch_shapes=[
            pltpu.VMEM((NM, 2, NB, RB, MW), F32),
            pltpu.VMEM((2, NB, RB, CB), F32),
            pltpu.VMEM((2 * CB, NB * RB), BF16),
            pltpu.VMEM((2 * CB, NB * RB), BF16),
            pltpu.VMEM((2, CB, OB), F32),
            pltpu.VMEM((NM, 2 * MW, OB), BF16),
            pltpu.VMEM((NM, 2 * MW, OB), BF16),
            pltpu.VMEM((NB * RB, 2 * MW), BF16),
            pltpu.VMEM((NB * RB, 2 * MW), BF16),
            pltpu.VMEM((NM, 2 * MW, 2 * CB), F32),
            pltpu.VMEM((NM, MW, 2 * CB), F32),
            pltpu.VMEM((NB, RB, OB), F32),
            pltpu.VMEM((NY, RB, OB), F32),
            pltpu.VMEM((NY, RB, OB), F32),
            pltpu.VMEM((NY - 1, RB, OB), F32),
            dma((NM, 2, NB)),
            dma((NM, 2)),
            dma((2, STEPS)),
            dma((2, NB)),
            dma((16,)),
            dma,
            dma((2,)),
            dma((NM,)),
            dma((NM,)),
            dma((NY,)),
            dma((NY,)),
            dma((NY - 1,)),
            dma((NY - 1,)),
        ],
        compiler_params=pltpu.CompilerParams(
            collective_id=0, has_side_effects=True, vmem_limit_bytes=56 * 2**20
        ),
        cost_estimate=pl.CostEstimate(flops=2 * 1610612736 * 3, bytes_accessed=4 * 2**20, transcendentals=0),
    )(basis, image, coeffs)


def solution(mesh):
    return jax.shard_map(
        on_device,
        mesh=mesh,
        in_specs=(P("row", "col"),) * 3,
        out_specs=(P("row", "col"),) * 3,
        check_vma=False,
    )
```

```python
import functools

import jax
import jax.numpy as jnp
from jax import lax
from jax.experimental import pallas as pl
from jax.experimental.pallas import tpu as pltpu
from jax.sharding import PartitionSpec as P

MESH = pl.DeviceIdType.MESH
F32, BF16 = jnp.float32, jnp.bfloat16
NY, NZ = 4, 8
RB, CB, OB = 256, 384, 256
NB = 8
NG, GW = 6, 64
UNIT = 4
UNITS = NG * NB // UNIT
LAG = 1
END = UNITS + 4 * LAG
R_NEAR, R_FAR = 7, 9
SHARED = 2


def halves(v):
    hi = v.astype(BF16)
    return hi, (v - hi.astype(F32)).astype(BF16)


def dot(a, b):
    return jnp.dot(a, b, preferred_element_type=F32)


def loop(lo, hi, body):
    def go(t, carry):
        body(t)
        return carry

    lax.fori_loop(lo, hi, go, 0)


def kernel(
    basis, image, coeffs, gram, stiff, rot,
    bt, lbuf, rbuf, r_hi, r_lo, cbuf, c_hi, c_lo, l_hi, l_lo, pbuf, precv, rotp, rotc, rots, roty,
    l_recv, l_send, z_send, x_send, r_recv, r_send, c_recv, c_send, p_recv, p_send, rc_recv, rc_send, ry_recv, ry_send,
):
    row, col = lax.axis_index("row"), lax.axis_index("col")
    xh, y, core = lax.div(row, 8), lax.rem(lax.div(row, 2), 4), lax.rem(row, 2)
    z, xl = lax.div(col, 2), lax.rem(col, 2)
    zs = lax.rem(z, 4)
    d = lax.rem(z - y + NZ, 4)
    own_blk = y * 2 + core
    lead = core == xl

    def dev(dxh=0, dxl=0, dy=0, dz=0, dc=0):
        a, b = lax.rem(xh + dxh, 2), lax.rem(xl + dxl, 2)
        return (a * 8 + lax.rem(y + dy + NY, NY) * 2 + lax.rem(core + dc, 2), lax.rem(z + dz + NZ, NZ) * 2 + b)

    other_core, partner, x_pair = dev(dc=1), dev(dxh=1), dev(dxl=1)
    y_up, y_dn, z_up, z_dn = dev(dy=1), dev(dy=-1), dev(dz=1), dev(dz=-1)

    def send(src, dst, s, r, to):
        return pltpu.make_async_remote_copy(
            src_ref=src, dst_ref=dst, send_sem=s, recv_sem=r, device_id=to, device_id_type=MESH
        )

    def arrived(dst, r):
        send(dst, dst, l_send.at[0], r, other_core).wait_recv()

    barrier = pltpu.get_barrier_semaphore()
    peers = [dev(dxl=a, dy=b, dc=c) for a in range(2) for b in range(4) for c in range(2) if a + b + c]
    peers += [z_up, z_dn, partner]
    for p in peers:
        pl.semaphore_signal(barrier, inc=1, device_id=p, device_id_type=MESH)
    own_in = [
        pltpu.make_async_copy(src, rbuf.at[arr, own_blk], r_recv.at[arr, own_blk])
        for arr, src in enumerate((basis, image))
    ]
    own_in.append(pltpu.make_async_copy(coeffs, cbuf.at[xh], c_send.at[1]))
    for cp in own_in:
        cp.start()
    own_in[0].wait()
    bt[...] = rbuf[0, own_blk].T
    own_in[1].wait()
    pl.semaphore_wait(barrier, len(peers))

    def blk_of(dy, c):
        return lax.rem(y + dy, NY) * 2 + c

    dy_src = lax.rem(y - zs + NY, NY)
    shared_src = ((dy_src == 1) | (dy_src == 2)) & (core == 0)
    mine = (y == zs) & lead

    def gather(g):
        src, dst, r = bt.at[pl.ds(g * GW, GW)], lbuf.at[0, own_blk, pl.ds(g * GW, GW)], l_recv.at[g, 0, own_blk]
        to = (xh * 8 + zs * 2 + xl, z * 2 + xl)
        pl.when(mine)(pltpu.make_async_copy(src, dst, r).start)
        pl.when(jnp.logical_not(mine))(send(src, dst, l_send.at[0], r, to).start)
        to = (xh * 8 + zs * 2 + xl, z * 2 + 1 - xl)
        if g < NG - 1:
            pl.when(jnp.logical_not(shared_src))(send(src, dst, l_send.at[1], r, to).start)
        else:
            send(src, dst, l_send.at[1], r, to).start()

    sends = []

    def r_go(arr, blk, to):
        at = rbuf.at[arr, blk]
        cp = send(at, at, r_send.at[len(sends)], r_recv.at[arr, blk], to)
        cp.start()
        sends.append(cp)

    def r_start(arr):
        r_go(arr, own_blk, y_up)
        r_go(arr, own_blk, y_dn)
        r_go(arr, own_blk, other_core)

    c_cp = send(coeffs, cbuf.at[xh], c_send.at[0], c_recv, partner)
    gather(0)
    gather(1)
    r_start(0)
    gather(2)
    r_start(1)
    gather(3)
    gather(4)
    gather(5)
    c_cp.start()

    def chunk_ref(g, slot, blk):
        return lbuf.at[slot, blk, pl.ds(pl.multiple_of(g * GW, GW), GW)]

    def pass_on(u, k, slot):
        g, half = lax.div(u, 2), lax.rem(u, 2)
        c = k % 2
        blk = blk_of(jnp.where(half == 0, k // 2, 3 - k // 2), c)
        src = chunk_ref(g, slot, blk)

        def along_z(up):
            into = jnp.where(d == 3, 1, 0) if up else 1
            send(
                src, chunk_ref(g, into, blk), z_send.at[0 if up else 1, g], l_recv.at[g, into, blk], z_up if up else z_dn
            ).start()

        def from_z():
            arrived(src, l_recv.at[g, slot, blk])
            if slot == 0:
                along_z(True) if c == 0 else pl.when(d < 3)(lambda: along_z(True))
                pl.when(d == 0)(lambda: along_z(False))
            else:
                pl.when((d > 1) | (d == 1) if c == 1 else d > 1)(lambda: along_z(False))

        if k == SHARED:
            pl.when(lead | (g == NG - 1))(from_z)
            pl.when(lead & (g < NG - 1))(send(src, src, x_send.at[g], l_recv.at[g, slot, blk], x_pair).start)
        else:
            from_z()

    def step(t, k):
        ua, ub = t - LAG * d, t - LAG * (4 - d)
        pl.when((ua >= 0) & (ua < UNITS))(lambda: pass_on(ua, k, 0))
        pl.when((ub >= 0) & (ub < UNITS))(lambda: pass_on(ub, k, 1))

    def unit(t):
        for k in range(UNIT):
            step(t, k)

    def sent(n, s):
        at = lbuf.at[0, pl.ds(0, n), pl.ds(0, GW)]
        send(at, at, s, l_recv.at[0, 0, 0], other_core).wait_send()

    def drain():
        for g in range(NG):
            few = g < NG - 1
            for up in (True, False):
                s = z_send.at[0 if up else 1, g]
                part = d == 3 if up else d == 1
                whole = jnp.logical_not(part)
                if few:
                    pl.when(whole & lead)(lambda: sent(8, s))
                    pl.when(whole & jnp.logical_not(lead))(lambda: sent(6, s))
                else:
                    pl.when(whole)(lambda: sent(8, s))
                if few and up:
                    pl.when(part & lead)(lambda: sent(4, s))
                    pl.when(part & jnp.logical_not(lead))(lambda: sent(2, s))
                else:
                    pl.when(part)(lambda: sent(4, s))
            if few:
                pl.when(lead)(lambda: sent(4, x_send.at[g]))

    own = jnp.where(lax.div(lax.rem(z - d + NZ, NZ), 4) == xh, 0, 1)
    h_a = jnp.where(own == 0, xh, 1 - xh)

    def split_r(blk, wait=True):
        for arr in range(2):
            if wait:
                arrived(rbuf.at[arr, blk], r_recv.at[arr, blk])
            hi, lo = halves(rbuf[arr, blk])
            at = (pl.ds(pl.multiple_of(blk * RB, RB), RB), pl.ds(arr * CB, CB))
            r_hi[at] = hi
            r_lo[at] = lo

    def split_c():
        own_in[2].wait()
        arrived(cbuf.at[1 - xh], c_recv)
        for g in range(NG):
            rows = pl.ds(g * GW, GW)
            both = jnp.concatenate([cbuf[h_a, rows, :], cbuf[1 - h_a, rows, :]], axis=0)
            hi, lo = halves(both.T)
            c_hi[:, pl.ds(g * 2 * GW, 2 * GW)] = hi
            c_lo[:, pl.ds(g * 2 * GW, 2 * GW)] = lo

    def shared_arrived(g):
        @pl.when(jnp.logical_not(lead))
        def _():
            for dy in (1, 2):
                blk = blk_of(dy, 0)
                for slot in range(2):
                    arrived(chunk_ref(g, slot, blk), l_recv.at[g, slot, blk])

    def split_l(groups, blks):
        for b in blks:
            cols = pl.ds(b * RB, RB)
            for k, g in enumerate(groups):
                for slot in range(2):
                    hi, lo = halves(lbuf[slot, b, pl.ds(g * GW, GW), :])
                    rows = pl.ds((k * 2 + slot) * GW, GW)
                    l_hi[rows, cols] = hi
                    l_lo[rows, cols] = lo

    def grams(groups, n):
        cols, rows = pl.ds(n * 256, 256), pl.ds(0, len(groups) * 2 * GW)
        a_hi, b_hi = l_hi[rows, :], r_hi[:, cols]
        acc = dot(a_hi, b_hi) + dot(l_lo[rows, :], b_hi) + dot(a_hi, r_lo[:, cols])
        for k, g in enumerate(groups):
            for slot in range(2):
                at = (k * 2 + slot) * GW
                pbuf[g, slot, :, cols] = acc[at : at + GW, :]

    def grams_part(g, n, part, dys):
        cols, rows, acc = pl.ds(n * 256, 256), pl.ds(0, 2 * GW), 0.0
        for dy in dys:
            ks = pl.ds(pl.multiple_of(lax.rem(y + dy, NY) * 2 * RB, 2 * RB), 2 * RB)
            a_hi, b_hi = l_hi[rows, ks], r_hi[ks, cols]
            acc += dot(a_hi, b_hi) + dot(l_lo[rows, ks], b_hi) + dot(a_hi, r_lo[ks, cols])
        for slot in range(2):
            v = acc[slot * GW : slot * GW + GW, :]
            pbuf[g, slot, :, cols] = v if part == 0 else pbuf[g, slot, :, cols] + v

    def split_part(g, dys):
        for dy in dys:
            for c in range(2):
                b = blk_of(dy, c)
                cols = pl.ds(pl.multiple_of(b * RB, RB), RB)
                for slot in range(2):
                    hi, lo = halves(lbuf[slot, b, pl.ds(g * GW, GW), :])
                    l_hi[pl.ds(slot * GW, GW), cols] = hi
                    l_lo[pl.ds(slot * GW, GW), cols] = lo

    def rotate_part(g, dys):
        rows, ks = pl.ds(0, 2 * GW), pl.ds(g * 2 * GW, 2 * GW)
        for dy in dys:
            for c in range(2):
                b = blk_of(dy, c)
                cols = pl.ds(pl.multiple_of(b * RB, RB), RB)
                b_hi, b_lo = l_hi[rows, cols], l_lo[rows, cols]
                rotp[b] += dot(c_hi[:, ks], b_hi) + dot(c_lo[:, ks], b_hi) + dot(c_hi[:, ks], b_lo)

    def p_copy(g):
        return send(pbuf.at[g, 1 - own], precv.at[g], p_send.at[g], p_recv.at[g], partner)

    def rotate(groups, blks):
        rows = pl.ds(0, len(groups) * 2 * GW)
        ks = pl.ds(groups[0] * 2 * GW, len(groups) * 2 * GW)
        for b in blks:
            cols = pl.ds(b * RB, RB)
            b_hi, b_lo = l_hi[rows, cols], l_lo[rows, cols]
            acc = dot(c_hi[:, ks], b_hi) + dot(c_lo[:, ks], b_hi) + dot(c_hi[:, ks], b_lo)
            rotp[b] = acc if groups[0] == 0 else rotp[b] + acc

    def p_go(groups):
        for g in groups:
            p_copy(g).start()

    def r_near():
        for arr in range(2):
            for dy in (1, 3):
                blk = blk_of(dy, core)
                arrived(rbuf.at[arr, blk], r_recv.at[arr, blk])
                r_go(arr, blk, other_core)
                if (arr, dy) == (0, 3):
                    r_go(arr, blk, y_up)
                if (arr, dy) == (1, 1):
                    r_go(arr, blk, y_dn)

    def r_far():
        blk = blk_of(2, core)
        for arr in range(2):
            arrived(rbuf.at[arr, blk], r_recv.at[arr, blk])
            r_go(arr, blk, other_core)

    rc, ry = {}, {}

    def rc_go(dys):
        for dy in dys:
            b = lax.rem(y + dy, NY)
            rc[dy] = send(rotp.at[b * 2 + 1 - core], rotc.at[b], rc_send.at[dy], rc_recv.at[dy], other_core)
            rc[dy].start()

    def ry_go(dys):
        for dy in dys:
            rc[dy].wait()
            b = lax.rem(y + dy, NY)
            rots[b] = rotp[b * 2 + core] + rotc[b]
            if dy:
                ry[dy] = send(rots.at[b], roty.at[dy - 1], ry_send.at[dy - 1], ry_recv.at[dy - 1], dev(dy=dy))
                ry[dy].start()

    def pair_work(groups):
        yield lambda: [shared_arrived(g) for g in groups if g < NG - 1] and split_l(groups, range(4))
        yield lambda: split_l(groups, range(4, 8))
        yield lambda: grams(groups, 0)
        yield lambda: grams(groups, 1)
        yield lambda: grams(groups, 2)
        yield lambda: p_go(groups)
        yield lambda: rotate(groups, range(4))
        yield lambda: rotate(groups, range(4, 8))

    plan = {}

    def at(t, *work):
        n = t * UNIT
        for w in work:
            while n in plan:
                n += 1
            plan[n] = w

    at(
        R_NEAR,
        r_near,
        lambda: split_r(blk_of(0, core), False),
        lambda: split_r(blk_of(0, 1 - core)),
        lambda: split_r(blk_of(1, core), False),
        lambda: split_r(blk_of(3, core), False),
        lambda: split_r(blk_of(1, 1 - core)),
        lambda: split_r(blk_of(3, 1 - core)),
        split_c,
    )
    at(R_FAR, r_far, lambda: split_r(blk_of(2, core), False), lambda: split_r(blk_of(2, 1 - core)))
    at(max(R_FAR, 4 + 4 * LAG), *pair_work((0, 1)))
    at(8 + 4 * LAG, *pair_work((2, 3)))
    at(10 + 4 * LAG, *pair_work((4,)))
    first, second = (0, 1), (3, 2)
    at(
        11 + 4 * LAG,
        lambda: split_part(5, first),
        lambda: rotate_part(5, first),
        lambda: [rc_go(first), grams_part(5, 0, 0, first)],
        lambda: [ry_go(first), grams_part(5, 1, 0, first)],
    )
    loop(0, R_NEAR, unit)
    for n in range(R_NEAR * UNIT, END * UNIT):
        step(jnp.int32(n // UNIT), n % UNIT)
        if n in plan:
            plan.pop(n)()
    for n in sorted(plan):
        plan[n]()

    grams_part(5, 2, 0, first)
    split_part(5, second)
    rotate_part(5, second)
    rc_go(second)
    grams_part(5, 0, 1, second)
    ry_go((2, 3))
    grams_part(5, 1, 1, second)
    grams_part(5, 2, 1, second)
    p_go((5,))

    for g in range(NG):
        if g == NG - 1:
            for cp in ry.values():
                cp.wait()
            rot[...] = (rots[y] + roty[0] + roty[1] + roty[2]).T
        p_copy(g).wait()
        rows = pl.ds(g * GW, GW)
        gram[rows, :] = pbuf[g, own, :, pl.ds(0, CB)] + precv[g, :, pl.ds(0, CB)]
        stiff[rows, :] = pbuf[g, own, :, pl.ds(CB, CB)] + precv[g, :, pl.ds(CB, CB)]

    pl.when(jnp.logical_not(mine))(send(bt, bt, l_send.at[0], c_recv, other_core).wait_send)
    pl.when(jnp.logical_not(shared_src))(send(bt, bt, l_send.at[1], c_recv, other_core).wait_send)
    last = bt.at[pl.ds(0, GW)]
    pl.when(shared_src)(send(last, last, l_send.at[1], c_recv, other_core).wait_send)
    for cp in sends:
        cp.wait_send()
    c_cp.wait_send()

    drain()


def on_device(basis, image, coeffs):
    dma = pltpu.SemaphoreType.DMA
    return pl.pallas_call(
        kernel,
        out_shape=[
            jax.ShapeDtypeStruct((CB, CB), F32),
            jax.ShapeDtypeStruct((CB, CB), F32),
            jax.ShapeDtypeStruct((RB, OB), F32),
        ],
        in_specs=[pl.BlockSpec(memory_space=pl.ANY)] * 3,
        out_specs=[pl.BlockSpec(memory_space=pltpu.VMEM)] * 3,
        scratch_shapes=[
            pltpu.VMEM((CB, RB), F32),
            pltpu.VMEM((2, NB, CB, RB), F32),
            pltpu.VMEM((2, NB, RB, CB), F32),
            pltpu.VMEM((NB * RB, 2 * CB), BF16),
            pltpu.VMEM((NB * RB, 2 * CB), BF16),
            pltpu.VMEM((2, CB, OB), F32),
            pltpu.VMEM((OB, 2 * CB), BF16),
            pltpu.VMEM((OB, 2 * CB), BF16),
            pltpu.VMEM((4 * GW, NB * RB), BF16),
            pltpu.VMEM((4 * GW, NB * RB), BF16),
            pltpu.VMEM((NG, 2, GW, 2 * CB), F32),
            pltpu.VMEM((NG, GW, 2 * CB), F32),
            pltpu.VMEM((NB, OB, RB), F32),
            pltpu.VMEM((NY, OB, RB), F32),
            pltpu.VMEM((NY, OB, RB), F32),
            pltpu.VMEM((NY - 1, OB, RB), F32),
            dma((NG, 2, NB)),
            dma((2,)),
            dma((2, NG)),
            dma((NG,)),
            dma((2, NB)),
            dma((16,)),
            dma,
            dma((2,)),
            dma((NG,)),
            dma((NG,)),
            dma((NY,)),
            dma((NY,)),
            dma((NY - 1,)),
            dma((NY - 1,)),
        ],
        compiler_params=pltpu.CompilerParams(
            collective_id=0, has_side_effects=True, vmem_limit_bytes=56 * 2**20
        ),
        cost_estimate=pl.CostEstimate(flops=2 * 1610612736 * 3, bytes_accessed=4 * 2**20, transcendentals=0),
    )(basis, image, coeffs)


def solution(mesh):
    return jax.shard_map(
        on_device,
        mesh=mesh,
        in_specs=(P("row", "col"),) * 3,
        out_specs=(P("row", "col"),) * 3,
        check_vma=False,
    )
```

```python
import functools

import jax
import jax.numpy as jnp
from jax import lax
from jax.experimental import pallas as pl
from jax.experimental.pallas import tpu as pltpu
from jax.sharding import PartitionSpec as P

MESH = pl.DeviceIdType.MESH
F32, BF16 = jnp.float32, jnp.bfloat16
NY, NZ = 4, 8
RB, CB, OB = 256, 384, 256
NB = 8
NG, GW = 6, 64
UNIT = 2
UNITS = NG * NB // UNIT
LAG, LAG_END = 3, 11
END = UNITS + LAG_END
R_NEAR, R_FAR = 14, 19
RATE = 8
PIECES = 11
NS = 4
SHARED = 0


def halves(v):
    hi = v.astype(BF16)
    return hi, (v - hi.astype(F32)).astype(BF16)


def dot(a, b):
    return jnp.dot(a, b, preferred_element_type=F32)


def loop(lo, hi, body):
    def go(t, carry):
        body(t)
        return carry

    lax.fori_loop(lo, hi, go, 0)


def kernel(
    basis, image, coeffs, gram, stiff, rot,
    bt, lbuf, rbuf, r_hi, r_lo, cbuf, c_hi, c_lo, l_hi, l_lo, pbuf, precv, rotp, rotc, rots, roty,
    l_recv, l_send, z_send, x_send, r_recv, r_send, c_recv, c_send, p_recv, p_send, rc_recv, rc_send, ry_recv, ry_send,
):
    row, col = lax.axis_index("row"), lax.axis_index("col")
    xh, y, core = lax.div(row, 8), lax.rem(lax.div(row, 2), 4), lax.rem(row, 2)
    z, xl = lax.div(col, 2), lax.rem(col, 2)
    zs = lax.rem(z, 4)
    d = lax.rem(z - y + NZ, 4)
    own_blk = y * 2 + core
    lead = core == xl

    def dev(dxh=0, dxl=0, dy=0, dz=0, dc=0):
        a, b = lax.rem(xh + dxh, 2), lax.rem(xl + dxl, 2)
        return (a * 8 + lax.rem(y + dy + NY, NY) * 2 + lax.rem(core + dc, 2), lax.rem(z + dz + NZ, NZ) * 2 + b)

    other_core, partner, x_pair = dev(dc=1), dev(dxh=1), dev(dxl=1)
    y_up, y_dn, z_up, z_dn = dev(dy=1), dev(dy=-1), dev(dz=1), dev(dz=-1)

    def send(src, dst, s, r, to):
        return pltpu.make_async_remote_copy(
            src_ref=src, dst_ref=dst, send_sem=s, recv_sem=r, device_id=to, device_id_type=MESH
        )

    def arrived(dst, r):
        send(dst, dst, l_send.at[0], r, other_core).wait_recv()

    barrier = pltpu.get_barrier_semaphore()
    peers = [dev(dxl=a, dy=b, dc=c) for a in range(2) for b in range(4) for c in range(2) if a + b + c]
    peers += [z_up, z_dn, partner]
    for p in peers:
        pl.semaphore_signal(barrier, inc=1, device_id=p, device_id_type=MESH)
    own_in = [
        pltpu.make_async_copy(src, rbuf.at[arr, own_blk], r_recv.at[arr, own_blk])
        for arr, src in enumerate((basis, image))
    ]
    own_in.append(pltpu.make_async_copy(coeffs, cbuf.at[xh], c_send.at[1]))
    for cp in own_in:
        cp.start()
    own_in[0].wait()
    bt[...] = rbuf[0, own_blk].T
    own_in[1].wait()
    pl.semaphore_wait(barrier, len(peers))

    def blk_of(dy, c):
        return lax.rem(y + dy, NY) * 2 + c

    mine = (y == zs) & lead

    def gather(g):
        src, dst, r = bt.at[pl.ds(g * GW, GW)], lbuf.at[0, own_blk, pl.ds(g * GW, GW)], l_recv.at[g, 0, own_blk]
        to = (xh * 8 + zs * 2 + xl, z * 2 + xl)
        pl.when(mine)(pltpu.make_async_copy(src, dst, r).start)
        pl.when(jnp.logical_not(mine))(send(src, dst, l_send.at[0], r, to).start)

    sends = []

    def r_go(arr, blk, to):
        at = rbuf.at[arr, blk]
        cp = send(at, at, r_send.at[len(sends)], r_recv.at[arr, blk], to)
        cp.start()
        sends.append(cp)

    def r_start(arr):
        r_go(arr, own_blk, y_up)
        r_go(arr, own_blk, y_dn)
        r_go(arr, own_blk, other_core)

    c_cp = send(coeffs, cbuf.at[xh], c_send.at[0], c_recv, partner)
    gather(0)
    gather(1)
    r_start(0)
    gather(2)
    r_start(1)
    gather(3)
    gather(4)
    gather(5)
    c_cp.start()

    def chunk_ref(g, slot, blk):
        return lbuf.at[slot, blk, pl.ds(pl.multiple_of(g * GW, GW), GW)]

    def pass_on(u, k, slot):
        g, part = lax.div(u, 4), lax.rem(u, 4)
        c = k % 2
        blk = blk_of(jnp.where(part == 2, 3, jnp.where(part == 3, 2, part)), c)
        src = chunk_ref(g, slot, blk)

        def along_z(up):
            into = jnp.where(d == 3, 1, 0) if up else 1
            send(
                src, chunk_ref(g, into, blk), z_send.at[0 if up else 1, g], l_recv.at[g, into, blk], z_up if up else z_dn
            ).start()

        def from_z():
            arrived(src, l_recv.at[g, slot, blk])
            if slot == 0:
                along_z(True) if c == 0 else pl.when(d < 3)(lambda: along_z(True))
                pl.when(d == 0)(lambda: along_z(False))
            else:
                pl.when((d > 1) | (d == 1) if c == 1 else d > 1)(lambda: along_z(False))

        shared = (g < NS) & ((part == 1) | (part == 3)) & (k == SHARED)
        if k == SHARED:
            pl.when(lead | jnp.logical_not(shared))(from_z)
        else:
            from_z()
        over = shared | (d == 0) if slot == 0 else shared
        if slot == 0 or k == SHARED:
            pl.when(lead & over)(send(src, src, x_send.at[g], l_recv.at[g, slot, blk], x_pair).start)

    lag_b = jnp.where(d == 0, LAG_END, LAG * (4 - d))

    def step(t, k):
        ua, ub = t - LAG * d, t - lag_b
        pl.when((ua >= 0) & (ua < UNITS))(lambda: pass_on(ua, k, 0))
        pl.when((ub >= 0) & (ub < UNITS))(lambda: pass_on(ub, k, 1))

    def unit(t):
        for k in range(UNIT):
            step(t, k)

    def sent(n, s):
        at = lbuf.at[0, pl.ds(0, n), pl.ds(0, GW)]
        send(at, at, s, l_recv.at[0, 0, 0], other_core).wait_send()

    def drain():
        for g in range(NG):
            few = g < NS
            for up in (True, False):
                s = z_send.at[0 if up else 1, g]
                part = d == 3 if up else d == 1
                whole = jnp.logical_not(part)
                if few:
                    pl.when(whole & lead)(lambda: sent(8, s))
                    pl.when(whole & jnp.logical_not(lead))(lambda: sent(6, s))
                else:
                    pl.when(whole)(lambda: sent(8, s))
                if few and up:
                    pl.when(part & lead)(lambda: sent(4, s))
                    pl.when(part & jnp.logical_not(lead))(lambda: sent(2, s))
                else:
                    pl.when(part)(lambda: sent(4, s))
            s = x_send.at[g]
            if few:
                pl.when(lead & (d > 0))(lambda: sent(4, s))

                at = lbuf.at[0, pl.ds(0, 5), pl.ds(0, 2 * GW)]
                pl.when(lead & (d == 0))(send(at, at, s, l_recv.at[0, 0, 0], other_core).wait_send)
            else:
                pl.when(lead & (d == 0))(lambda: sent(8, s))


    own = jnp.where(lax.div(lax.rem(z - d + NZ, NZ), 4) == xh, 0, 1)
    h_a = jnp.where(own == 0, xh, 1 - xh)

    def split_r(blk, wait=True):
        for arr in range(2):
            if wait:
                arrived(rbuf.at[arr, blk], r_recv.at[arr, blk])
            hi, lo = halves(rbuf[arr, blk])
            at = (pl.ds(pl.multiple_of(blk * RB, RB), RB), pl.ds(arr * CB, CB))
            r_hi[at] = hi
            r_lo[at] = lo

    def split_c():
        own_in[2].wait()
        arrived(cbuf.at[1 - xh], c_recv)
        for g in range(NG):
            rows = pl.ds(g * GW, GW)
            both = jnp.concatenate([cbuf[h_a, rows, :], cbuf[1 - h_a, rows, :]], axis=0)
            hi, lo = halves(both.T)
            c_hi[:, pl.ds(g * 2 * GW, 2 * GW)] = hi
            c_lo[:, pl.ds(g * 2 * GW, 2 * GW)] = lo

    def shared_arrived(g):
        @pl.when(jnp.logical_not(lead))
        def _():
            for dy in (1, 2):
                blk = blk_of(dy, 0)
                for slot in range(2):
                    arrived(chunk_ref(g, slot, blk), l_recv.at[g, slot, blk])

    def split_l(g, b):
        cols, at = pl.ds(pl.multiple_of(b * RB, RB), RB), pl.ds(pl.multiple_of(g * GW, GW), GW)
        for slot in range(2):
            hi, lo = halves(lbuf[slot, b, at, :])
            l_hi[pl.ds(slot * GW, GW), cols] = hi
            l_lo[pl.ds(slot * GW, GW), cols] = lo

    def grams(g, n):
        cols = pl.ds(pl.multiple_of(n * 256, 256), 256)
        b_hi = r_hi[:, cols]
        acc = dot(l_hi[...], b_hi) + dot(l_lo[...], b_hi) + dot(l_hi[...], r_lo[:, cols])
        for slot in range(2):
            pbuf[g, slot, :, cols] = acc[slot * GW : slot * GW + GW, :]

    def rotate(g, b):
        cols, ks = pl.ds(pl.multiple_of(b * RB, RB), RB), pl.ds(pl.multiple_of(g * 2 * GW, 2 * GW), 2 * GW)
        b_hi, b_lo, a_hi = l_hi[:, cols], l_lo[:, cols], c_hi[:, ks]
        rotp[b] += dot(a_hi, b_hi) + dot(c_lo[:, ks], b_hi) + dot(a_hi, b_lo)

    def piece(i):
        g, r = lax.div(i, PIECES), lax.rem(i, PIECES)
        pl.when((r == 0) & (g < NS))(lambda: shared_arrived(g))

        @pl.when(r < 4)
        def _():
            for c in range(2):
                split_l(g, r * 2 + c)

        pl.when((r >= 4) & (r < 7))(lambda: grams(g, r - 4))
        pl.when(r == 6)(lambda: p_copy(g).start())

        @pl.when(r >= 7)
        def _():
            for c in range(2):
                rotate(g, (r - 7) * 2 + c)

    def p_copy(g):
        return send(pbuf.at[g, 1 - own], precv.at[g], p_send.at[g], p_recv.at[g], partner)

    def r_near():
        for arr in range(2):
            for dy in (1, 3):
                blk = blk_of(dy, core)
                arrived(rbuf.at[arr, blk], r_recv.at[arr, blk])
                r_go(arr, blk, other_core)
                if (arr, dy) == (0, 3):
                    r_go(arr, blk, y_up)
                if (arr, dy) == (1, 1):
                    r_go(arr, blk, y_dn)

    def r_far():
        blk = blk_of(2, core)
        for arr in range(2):
            arrived(rbuf.at[arr, blk], r_recv.at[arr, blk])
            r_go(arr, blk, other_core)

    rc, ry = {}, {}

    def rc_go(dys):
        for dy in dys:
            b = lax.rem(y + dy, NY)
            rc[dy] = send(rotp.at[b * 2 + 1 - core], rotc.at[b], rc_send.at[dy], rc_recv.at[dy], other_core)
            rc[dy].start()

    def ry_go(dys):
        for dy in dys:
            rc[dy].wait()
            b = lax.rem(y + dy, NY)
            rots[b] = rotp[b * 2 + core] + rotc[b]
            if dy:
                ry[dy] = send(rots.at[b], roty.at[dy - 1], ry_send.at[dy - 1], ry_recv.at[dy - 1], dev(dy=dy))
                ry[dy].start()

    rotp[...] = jnp.zeros_like(rotp)
    loop(0, R_NEAR, unit)
    r_near()

    def with_own(t):
        unit(t)
        i = t - R_NEAR
        split_r(blk_of(jnp.where(i == 2, 3, i), core), False)

    def with_other(t):
        unit(t)
        split_r(blk_of(t - (R_NEAR + 3), 1 - core))

    loop(R_NEAR, R_NEAR + 3, with_own)
    loop(R_NEAR + 3, R_FAR, with_other)
    r_far()
    unit(jnp.int32(R_FAR))
    split_r(blk_of(3, 1 - core))
    split_c()
    unit(jnp.int32(R_FAR + 1))
    split_r(blk_of(2, core), False)
    split_r(blk_of(2, 1 - core))

    def with_work(t):
        unit(t)
        i = t - (R_FAR + 2)
        most = (NG - 1) * PIECES
        loop(jnp.minimum(lax.div(i * RATE, 2), most), jnp.minimum(lax.div((i + 1) * RATE, 2), most), piece)

    loop(R_FAR + 2, END, with_work)

    last = NG - 1
    loop(min((END - R_FAR - 2) * RATE // 2, last * PIECES), last * PIECES, piece)
    loop(0, NB, lambda b: split_l(last, b))
    loop(0, NB, lambda b: rotate(last, b))
    rc_go(range(NY))
    loop(0, 2, lambda n: grams(last, n))
    ry_go((2, 1, 3, 0))
    grams(last, 2)
    p_copy(last).start()

    for g in range(NG):
        if g == NG - 1:
            for cp in ry.values():
                cp.wait()
            rot[...] = (rots[y] + roty[0] + roty[1] + roty[2]).T
        p_copy(g).wait()
        rows = pl.ds(g * GW, GW)
        gram[rows, :] = pbuf[g, own, :, pl.ds(0, CB)] + precv[g, :, pl.ds(0, CB)]
        stiff[rows, :] = pbuf[g, own, :, pl.ds(CB, CB)] + precv[g, :, pl.ds(CB, CB)]

    pl.when(jnp.logical_not(mine))(send(bt, bt, l_send.at[0], c_recv, other_core).wait_send)
    for cp in sends:
        cp.wait_send()
    c_cp.wait_send()

    drain()


def on_device(basis, image, coeffs):
    dma = pltpu.SemaphoreType.DMA
    return pl.pallas_call(
        kernel,
        out_shape=[
            jax.ShapeDtypeStruct((CB, CB), F32),
            jax.ShapeDtypeStruct((CB, CB), F32),
            jax.ShapeDtypeStruct((RB, OB), F32),
        ],
        in_specs=[pl.BlockSpec(memory_space=pl.ANY)] * 3,
        out_specs=[pl.BlockSpec(memory_space=pltpu.VMEM)] * 3,
        scratch_shapes=[
            pltpu.VMEM((CB, RB), F32),
            pltpu.VMEM((2, NB, CB, RB), F32),
            pltpu.VMEM((2, NB, RB, CB), F32),
            pltpu.VMEM((NB * RB, 2 * CB), BF16),
            pltpu.VMEM((NB * RB, 2 * CB), BF16),
            pltpu.VMEM((2, CB, OB), F32),
            pltpu.VMEM((OB, 2 * CB), BF16),
            pltpu.VMEM((OB, 2 * CB), BF16),
            pltpu.VMEM((2 * GW, NB * RB), BF16),
            pltpu.VMEM((2 * GW, NB * RB), BF16),
            pltpu.VMEM((NG, 2, GW, 2 * CB), F32),
            pltpu.VMEM((NG, GW, 2 * CB), F32),
            pltpu.VMEM((NB, OB, RB), F32),
            pltpu.VMEM((NY, OB, RB), F32),
            pltpu.VMEM((NY, OB, RB), F32),
            pltpu.VMEM((NY - 1, OB, RB), F32),
            dma((NG, 2, NB)),
            dma((1,)),
            dma((2, NG)),
            dma((NG,)),
            dma((2, NB)),
            dma((16,)),
            dma,
            dma((2,)),
            dma((NG,)),
            dma((NG,)),
            dma((NY,)),
            dma((NY,)),
            dma((NY - 1,)),
            dma((NY - 1,)),
        ],
        compiler_params=pltpu.CompilerParams(
            collective_id=0, has_side_effects=True, vmem_limit_bytes=56 * 2**20
        ),
        cost_estimate=pl.CostEstimate(flops=2 * 1610612736 * 3, bytes_accessed=4 * 2**20, transcendentals=0),
    )(basis, image, coeffs)


def solution(mesh):
    return jax.shard_map(
        on_device,
        mesh=mesh,
        in_specs=(P("row", "col"),) * 3,
        out_specs=(P("row", "col"),) * 3,
        check_vma=False,
    )
```
